256 devices in a mesh: patch: 64 (over z_hi, y, x), head: 4 (over z_lo, core).
Axes of the slice: x: 4, y: 4, z: 8 (z_hi: 4, z_lo: 2; z = z_hi * 2 + z_lo), core: 2. Of those that a mesh axis runs over, the one named last changes fastest.
Arguments:
- fresh_qkv: bfloat16 [2, 8192, 3, 1536], P(None, ('patch', 'head'))
- stale_kv: bfloat16 [8192, 2, 1536], P('patch', None, 'head'), may hold values from -8 to 8
- text_mask: int32 [256], replicated, may hold values 0 or 1
- out_weight: bfloat16 [1536, 3072], P('head'), may hold values from -0.15625 to 0.15625
- inputs: bfloat16 [2, 8192, 3072], P(None, ('patch', 'head')), may hold values from -6 to 6
- gate: float32 [2, 3072], replicated, may hold values from -4 to 4
Outputs:
- blended: bfloat16 [2, 8192, 3072], P(None, ('patch', 'head'))
The draws below stay inside these ranges and needn't reach their ends.
All inputs are finite; a program needn't handle non-finite values.
Results may differ from the reference program's by a relative error of at most 0.014.
Values may be sent and summed in bfloat16 or wider, within the bound.
A program may use at most 128 MiB of HBM per device.

```python
import jax
import jax.numpy as jnp
from jax import lax

D = 3072
HEADS = 12
HEAD_DIM = 128
TXT = 256
STEPS = 2
PATCH_TOK = 128
TOKENS = 8192


def draw_fresh_qkv(key, part):
    key = jax.random.fold_in(key, 11)
    width = HEADS * HEAD_DIM
    shape = (STEPS, TOKENS, 3, width)
    return (1.7 * jnp.clip(jax.random.normal(key, shape, jnp.float32), -5.0, 5.0)).astype(jnp.bfloat16)


def with_ends(drawn, stream_key, low, top_value):
    index_at = [jax.random.randint(jax.random.fold_in(stream_key, axis), (), 0, length) for axis, length in enumerate(drawn.shape)]
    main_axis = drawn.shape.index(max(drawn.shape))
    neighbour = index_at[:main_axis] + [(index_at[main_axis] + 1) % drawn.shape[main_axis]] + index_at[main_axis + 1:]
    return drawn.at[tuple(index_at)].set(low).at[tuple(neighbour)].set(top_value)


def block_scale(key, dims, split, low, high):
    factor_of, own = 1.0, jax.random.fold_in(key, 6)
    for position, shards_of in split:
        heights = jnp.exp(jax.random.uniform(jax.random.fold_in(own, position), (shards_of,), jnp.float32, low / len(split), high / len(split)))
        factor_of = factor_of * jnp.repeat(heights, dims[position] // shards_of).reshape([-1 if axis == position else 1 for axis in range(len(dims))])
    return factor_of


def noise(own_key, extent, spread, reach, pieces=(), held_as=jnp.bfloat16):
    array = spread * jax.random.normal(own_key, extent, jnp.float32)
    if pieces:
        array = array * block_scale(own_key, extent, pieces, -0.22, 0.18)
    return jnp.clip(array, -reach, reach).astype(held_as)


def setup_inputs(seed: int = 0) -> dict:
    keys = jax.random.split(jax.random.key(seed), 7)
    return {
        "fresh_qkv": draw_fresh_qkv(jax.random.fold_in(keys[6], 71), 0),
        "stale_kv": noise(keys[1], (TOKENS, 2, HEADS * HEAD_DIM), 1.7, 8.0, ((0, 64), (2, 4))),
        "text_mask": with_ends((jax.random.randint(keys[2], (TXT,), 0, 4) < 3).astype(jnp.int32), jax.random.fold_in(keys[2], 1), 0, 1),
        "out_weight": noise(keys[3], (HEADS * HEAD_DIM, D), (HEADS * HEAD_DIM) ** -0.5, 0.15625, ((0, 4),)),
        "inputs": noise(keys[4], (STEPS, TOKENS, D), 1.0, 6.0, ((1, 256),)),
        "gate": noise(keys[5], (STEPS, D), 1.0, 4.0, (), jnp.float32),
    }


def attend_patch(queries, key_rows, value_rows, key_valid):
    scores = jnp.einsum("qhd,khd->hqk", queries.astype(jnp.float32), key_rows.astype(jnp.float32)) * (HEAD_DIM ** -0.5)
    scores = jnp.where(key_valid[None, None, :], scores, -1.0e30)
    row_top = jnp.max(scores, axis=2, keepdims=True)
    exps = jnp.where(key_valid[None, None, :], jnp.exp(scores - row_top), 0.0)
    row_total = jnp.sum(exps, axis=2)
    weights = exps.astype(jnp.bfloat16).astype(jnp.float32)
    summed = jnp.einsum("hqk,khd->qhd", weights, value_rows.astype(jnp.float32))
    return (summed / jnp.transpose(row_total)[:, :, None]).astype(jnp.bfloat16)


def reference(fresh_qkv, stale_kv, text_mask, out_weight, inputs, gate):
    patches = TOKENS // PATCH_TOK
    key_valid = jnp.concatenate([jnp.ones((TOKENS - TXT,), jnp.int32), text_mask]) == 1
    owner_patch = jnp.arange(TOKENS, dtype=jnp.int32) // PATCH_TOK
    stale_now = stale_kv
    results = []
    for step_index in range(STEPS):
        fresh_now = fresh_qkv[step_index]

        def one_patch(patch_index):
            first = (patch_index * PATCH_TOK).astype(jnp.int32)
            queries = lax.dynamic_slice_in_dim(fresh_now[:, 0], first, PATCH_TOK, 0)
            queries = queries.reshape(PATCH_TOK, HEADS, HEAD_DIM)
            in_patch = (owner_patch == patch_index)[:, None, None]
            key_value = jnp.where(in_patch, fresh_now[:, 1:3], stale_now)
            key_value = key_value.reshape(TOKENS, 2, HEADS, HEAD_DIM)
            return attend_patch(queries, key_value[:, 0], key_value[:, 1], key_valid)

        attended = lax.map(one_patch, jnp.arange(patches, dtype=jnp.int32))
        attended = attended.reshape(TOKENS, HEADS * HEAD_DIM)
        branch = jnp.dot(attended, out_weight, preferred_element_type=jnp.float32)
        blended = inputs[step_index].astype(jnp.float32) + gate[step_index][None, :] * branch
        results.append(blended.astype(jnp.bfloat16))
        stale_now = fresh_now[:, 1:3]
    return jnp.stack(results)
```

```python
import functools

import jax
import jax.numpy as jnp
from jax import lax
from jax.experimental import pallas as pl
from jax.experimental.pallas import tpu as pltpu
from jax.sharding import PartitionSpec as P

HEAD_DIM = 128
MESH = pl.DeviceIdType.MESH
MASKED = -1e30
SCALE = HEAD_DIM**-0.5 * 1.4426950408889634
BF16 = jnp.bfloat16
F32 = jnp.float32


def device(x, y, z, c):
    return ((z // 2) * 16 + y * 4 + x, (z % 2) * 2 + c)


def plane(z):
    return (z // 2) % 2, 2 * (z % 2) + z // 4


def columns_of(rows):
    count, width = rows.shape
    padded = jnp.concatenate([rows, jnp.zeros((128 - count, width), F32)], axis=0)
    return jnp.transpose(padded)


def as_row(column, width):
    return jnp.transpose(jnp.broadcast_to(column, (width, 128)))[:8]


def attend(queries, keys, values, add_bias):
    scores = lax.dot_general(queries, keys, (((1,), (1,)), ((), ())), preferred_element_type=F32)
    scores = add_bias(scores)
    best = jnp.max(scores, axis=1, keepdims=True) * SCALE
    exps = jnp.exp2(scores * SCALE - best)
    total = jnp.sum(exps, axis=1, keepdims=True)
    summed = jnp.dot(exps.astype(BF16), values, preferred_element_type=F32)
    return (summed / total).astype(BF16), best + jnp.log2(total)


def kernel(
    fresh, stale, mask, weight, inputs, gate, out,
    q, kv, part_out, part_in, stat_out, stat_in, merged, merged_stat, land, land_stat,
    home, own, own_out, own_stat, w_all, att, pair_out, pair_in, kept, bias_own, cols, cols_own,
    zq_s, zq_r, zk_s, zs_s, zk_r, home_s, home_r, w_s, w_r, w_l, xq_s, xq_r, qf_s, qf_r, yk_s, yk_r,
    o_s, o_r, t_s, t_r, b_s, b_r, bt_s, bt_r, own_s, own_r, ot_s, ot_r, p_s, p_r,
):
    patch, head = lax.axis_index("patch"), lax.axis_index("head")
    x, y, zh = patch % 4, (patch // 4) % 4, patch // 16
    zl, c = head // 2, head % 2
    z = zh * 2 + zl
    step_here, group_here = plane(z)
    slot_here = step_here * 2 + group_here % 2
    sibling = device(x, y, z, 1 - c)

    def send(src, dst, ss, rs, to):
        pltpu.make_async_remote_copy(
            src_ref=src, dst_ref=dst, send_sem=ss, recv_sem=rs, device_id=to, device_id_type=MESH
        ).start()

    def wait(ref, sem):
        pltpu.make_async_copy(ref, ref, sem).wait()

    barrier = pltpu.get_barrier_semaphore()

    def greet(to):
        pl.semaphore_signal(barrier, inc=1, device_id=to, device_id_type=MESH)

    greet(sibling)

    @pl.loop(1, 8)
    def _(d):
        greet(device(x, y, (z + d) % 8, 0))
        greet(device(x, y, (z + d) % 8, 1))

    @pl.loop(1, 4)
    def _(d):
        greet(device((x + d) % 4, y, z, 0))
        greet(device((x + d) % 4, y, z, 1))
        greet(device(x, (y + d) % 4, z, c))

    pl.semaphore_wait(barrier, 24)

    stale_plane = 4 * c + zl
    for h in range(3):
        for lane in range(2):
            src = stale.at[:, :, lane, :, pl.ds(h * 128, 128)]
            dst = kv.at[h, :, y, pl.ds(2 * zh, 2)]
            here = jnp.logical_and(stale_plane == z, c == lane)

            @pl.when(here)
            def _():
                pltpu.make_async_copy(src, dst, zk_r.at[h]).start()

            @pl.when(jnp.logical_not(here))
            def _():
                send(src, dst, zs_s.at[h], zk_r.at[h], device(x, y, stale_plane, lane))

        def piece(of_step, kind, group):
            first = pl.multiple_of(group * 384 + h * 128, 128)
            return fresh.at[of_step, kind, :, pl.ds(first, 128)]

        @pl.when(step_here == 1)
        def _():
            pltpu.make_async_copy(piece(0, slice(1, 3), group_here), kv.at[h, :, y, z], zk_r.at[h]).start()

        pltpu.make_async_copy(piece(step_here, 0, group_here), q.at[h, c, 0, z], zq_r.at[h]).start()

        @pl.loop(1, 8)
        def _(d):
            to_z = (z + d) % 8
            to_step, to_group = plane(to_z)
            to = device(x, y, to_z, c)

            @pl.when(to_step == 1)
            def _():
                send(piece(0, slice(1, 3), to_group), kv.at[h, :, y, z], zk_s.at[h], zk_r.at[h], to)

            send(piece(to_step, 0, to_group), q.at[h, c, 0, z], zq_s.at[h], zq_r.at[h], to)

    group = pl.multiple_of(head * 384, 128)
    pltpu.make_async_copy(fresh.at[:, :, :, pl.ds(group, 384)], home.at[:, :, c, zl], home_r.at[0]).start()

    @pl.loop(1, 4)
    def _(d):
        to_head = (head + d) % 4
        first = pl.multiple_of(to_head * 384, 128)
        send(fresh.at[:, :, :, pl.ds(first, 384)], home.at[:, :, c, zl], home_s.at[0], home_r.at[0], (patch, to_head))

    pltpu.make_async_copy(weight, w_all.at[c], w_l.at[0]).start()
    send(weight, w_all.at[c], w_s.at[0], w_r.at[0], sibling)

    mask_row = jnp.where(x == 3, mask[1:2, :], mask[0:1, :])
    text = jnp.where(mask_row == 1, 0.0, MASKED)
    lanes = lax.broadcasted_iota(jnp.int32, (1, 128), 1)
    by_32, by_64, by_96 = (jnp.roll(text, shift, axis=1) for shift in (32, 64, 96))
    low = jnp.where(lanes < 96, by_64, by_32)
    high = jnp.where(lanes < 96, by_32, text)
    text_keys = jnp.where(jnp.logical_and(x >= 2, lanes >= 64), jnp.where(c == 0, low, high), 0.0)
    own_order = jnp.where(lanes < 32, text, jnp.where(lanes < 64, by_96, jnp.where(lanes < 96, by_32, text)))
    own_bias = jnp.where(jnp.logical_and(x >= 2, jnp.logical_and(y == 3, zh == 3)), own_order, 0.0)

    bias_own[...] = jnp.zeros((256, 1024), F32)
    bias_own[:, 896:1024] = jnp.broadcast_to(text_keys, (256, 128))
    same = lax.broadcasted_iota(jnp.int32, (256, 256), 0) // 64 == lax.broadcasted_iota(jnp.int32, (256, 256), 1) // 64
    own_cols = pl.ds(pl.multiple_of(y * 256, 256), 256)
    bias_own[:, own_cols] = jnp.where(same, MASKED, bias_own[:, own_cols])

    for h in range(3):
        wait(kv.at[h, :, y], zk_r.at[h])

        @pl.loop(1, 4)
        def _(d):
            send(kv.at[h, :, y], kv.at[h, :, y], yk_s.at[h], yk_r.at[h, d - 1], device(x, (y + d) % 4, z, c))

        wait(q.at[h, c, 0], zq_r.at[h])

        @pl.loop(1, 4)
        def _(d):
            send(q.at[h, c, 0], q.at[h, c, 4 - d], xq_s.at[h], xq_r.at[h], device((x + d) % 4, y, z, c))

    wait(home, home_r.at[0])
    for s in range(2):
        for h in range(3):
            rows = [home[s, kind, :, :, :, h * 128 : h * 128 + 128].reshape(128, 128) for kind in range(3)]
            block, lse = attend(*rows, lambda scores: scores + own_bias)
            halves = block.reshape(2, 64, 128)
            own[c, s, h] = jnp.where(c == 0, halves[0], halves[1])
            own_out[s, h] = jnp.where(c == 0, halves[1], halves[0])
            own_stat[c, s * 3 + h : s * 3 + h + 1, :] = as_row(lse, 128)[:1]
    send(own_out, own.at[c], own_s.at[0], own_r.at[0], sibling)
    send(own_stat.at[c], own_stat.at[c], ot_s.at[0], ot_r.at[0], sibling)

    for h in range(3):
        wait(q.at[h, c, pl.ds(1, 3)], xq_r.at[h])
        send(q.at[h, c], q.at[h, c], qf_s.at[h], qf_r.at[h], sibling)

    for h in range(3):
        for d in range(1, 4):
            wait(kv.at[h, :, (y + 4 - d) % 4], yk_r.at[h, d - 1])
        wait(q.at[h, 1 - c], qf_r.at[h])

        def tile(r, lane, add_bias):
            keys, values = (kv[h, kind].reshape(1024, 128) for kind in range(2))
            return attend(q[h, lane, r].reshape(256, 128), keys, values, add_bias)

        def text_bias(scores):
            return jnp.concatenate([scores[:, :896], scores[:, 896:] + text_keys], axis=1)

        @pl.loop(2, 8)
        def _(index):
            r, lane = index // 2, index % 2
            block, lse = tile(r, lane, text_bias)
            part_out[h, index - 1] = block
            stat_out[h, index - 1] = as_row(lse, 256)
            to = device((x + r) % 4, y, z, lane)
            slot = (4 - r) * 2 + (c + lane) % 2
            send(part_out.at[h, index - 1], part_in.at[h, slot], o_s.at[h], o_r.at[h], to)
            send(stat_out.at[h, index - 1], stat_in.at[h, slot], t_s.at[h], t_r.at[h], to)

        block, lse = tile(0, 1 - c, lambda scores: scores + bias_own[...])
        part_out[h, 0] = block
        stat_out[h, 0] = as_row(lse, 256)
        send(part_out.at[h, 0], part_in.at[h, 1], o_s.at[h], o_r.at[h], sibling)
        send(stat_out.at[h, 0], stat_in.at[h, 1], t_s.at[h], t_r.at[h], sibling)
        block, lse = tile(0, c, lambda scores: scores + bias_own[...])
        part_in[h, 0] = block
        stat_in[h, 0] = as_row(lse, 256)

    for h in range(3):
        wait(part_in.at[h, pl.ds(1, 7)], o_r.at[h])
        wait(stat_in.at[h, pl.ds(1, 7)], t_r.at[h])
        stats = stat_in[h, :, 0, :]
        best = jnp.max(stats, axis=0, keepdims=True)
        shares = jnp.exp2(stats - best)
        total = jnp.sum(shares, axis=0, keepdims=True)
        share_cols = columns_of(shares / total)
        summed = part_in[h, 0].astype(F32) * share_cols[:, 0:1]
        for i in range(1, 8):
            summed = summed + part_in[h, i].astype(F32) * share_cols[:, i : i + 1]
        merged[h] = summed.astype(BF16).reshape(4, 64, 128)
        merged_stat[h] = jnp.broadcast_to(best + jnp.log2(total), (8, 256))
        pltpu.make_async_copy(merged.at[h, zh], land.at[h, slot_here], b_r.at[h]).start()
        pltpu.make_async_copy(merged_stat.at[h], land_stat.at[h, slot_here], bt_r.at[h]).start()

        @pl.loop(1, 4)
        def _(d):
            to_zh = (zh + d) % 4
            to = device(x, y, 2 * to_zh + zl, c)
            send(merged.at[h, to_zh], land.at[h, slot_here], b_s.at[h], b_r.at[h], to)
            send(merged_stat.at[h], land_stat.at[h, slot_here], bt_s.at[h], bt_r.at[h], to)

    wait(own_out, own_r.at[0])
    wait(own_stat.at[0], ot_r.at[0])
    cols_own[...] = columns_of(own_stat[...].reshape(16, 128))
    own_cols_here = cols_own[pl.ds(pl.multiple_of(c * 64, 64), 64), :]
    for h in range(3):
        wait(land.at[h], b_r.at[h])
        wait(land_stat.at[h], bt_r.at[h])
        cols[...] = columns_of(land_stat[h, :, 0, :])
        cols_here = cols[pl.ds(pl.multiple_of(zh * 64, 64), 64), :]
        for s in range(2):
            for j in range(2):
                lse_far = cols_here[:, s * 2 + j : s * 2 + j + 1]
                at = j * 8 + s * 3 + h
                lse_own = own_cols_here[:, at : at + 1]
                best = jnp.maximum(lse_far, lse_own)
                far, near = jnp.exp2(lse_far - best), jnp.exp2(lse_own - best)
                blended = (land[h, s * 2 + j].astype(F32) * far + own[j, s, h].astype(F32) * near) / (far + near)
                first = j * 384 + h * 128
                att[:, s * 32 : s * 32 + 32, first : first + 128] = blended.astype(BF16).reshape(2, 32, 128)

    wait(weight, w_l.at[0])
    wait(weight, w_r.at[0])
    pair = device(x, y, zh * 2 + 1 - zl, c)

    def project(which, n):
        cut = slice(n * 768, n * 768 + 768)
        return sum(
            jnp.dot(att[which, :, j * 384 : j * 384 + 384], w_all[j, :, cut], preferred_element_type=F32)
            for j in range(2)
        )

    for n in range(4):
        pair_out[n] = project(1 - zl, n).astype(BF16)
        send(pair_out.at[n], pair_in.at[n], p_s.at[n], p_r.at[n], pair)
    for n in range(4):
        kept[n] = project(zl, n)
    for n in range(4):
        wait(pair_in.at[n], p_r.at[n])
        cut = slice(n * 768, n * 768 + 768)
        branch = kept[n] + pair_in[n].astype(F32)
        for s in range(2):
            rows = slice(s * 32, s * 32 + 32)
            out[s, :, cut] = (inputs[s, :, cut].astype(F32) + gate[s : s + 1, cut] * branch[rows]).astype(BF16)

    for h in range(3):
        wait(q.at[h, 0, 0, pl.ds(0, 7)], zq_s.at[h])
        wait(q.at[h, 0, pl.ds(1, 3)], xq_s.at[h])
        wait(q.at[h, 0], qf_s.at[h])
        wait(kv.at[h, :, pl.ds(0, 3)], yk_s.at[h])
        wait(part_out.at[h, pl.ds(0, 7)], o_s.at[h])
        wait(stat_out.at[h, pl.ds(0, 7)], t_s.at[h])
        wait(merged.at[h, pl.ds(0, 3)], b_s.at[h])
        wait(land_stat.at[h, pl.ds(0, 3)], bt_s.at[h])

        @pl.when(step_here == 1)
        def _():
            wait(kv.at[h, :, 0, pl.ds(0, 3)], zk_s.at[h])

        @pl.when(step_here == 0)
        def _():
            wait(kv.at[h, :, 0, pl.ds(0, 4)], zk_s.at[h])

        @pl.when(stale_plane == z)
        def _():
            wait(kv.at[h, :, 0, pl.ds(0, 2)], zs_s.at[h])

        @pl.when(stale_plane != z)
        def _():
            wait(kv.at[h, :, 0, pl.ds(0, 4)], zs_s.at[h])

    wait(home.at[:, :, 0], home_s.at[0])
    wait(home.at[:, :, 0, 0], home_s.at[0])
    wait(weight, w_s.at[0])
    wait(own_out, own_s.at[0])
    wait(own_stat.at[0], ot_s.at[0])
    for n in range(4):
        wait(pair_out.at[n], p_s.at[n])


def shards(fresh_qkv, stale_kv, text_mask, out_weight, inputs, gate):
    fresh = jnp.transpose(fresh_qkv, (0, 2, 1, 3))
    stale = jnp.transpose(stale_kv, (1, 0, 2)).reshape(2, 2, 2, 32, 384)
    vmem, anywhere = pl.BlockSpec(memory_space=pltpu.VMEM), pl.BlockSpec(memory_space=pl.ANY)
    dma = pltpu.SemaphoreType.DMA
    sems = {
        "zq_s": (3,), "zq_r": (3,), "zk_s": (3,), "zs_s": (3,), "zk_r": (3,), "home_s": (1,), "home_r": (1,),
        "w_s": (1,), "w_r": (1,), "w_l": (1,), "xq_s": (3,), "xq_r": (3,), "qf_s": (3,), "qf_r": (3,),
        "yk_s": (3,), "yk_r": (3, 3), "o_s": (3,), "o_r": (3,), "t_s": (3,), "t_r": (3,), "b_s": (3,), "b_r": (3,),
        "bt_s": (3,), "bt_r": (3,), "own_s": (1,), "own_r": (1,), "ot_s": (1,), "ot_r": (1,), "p_s": (4,), "p_r": (4,),
    }
    buffers = {
        "q": ((3, 2, 4, 8, 32, 128), BF16), "kv": ((3, 2, 4, 8, 32, 128), BF16),
        "part_out": ((3, 7, 256, 128), BF16), "part_in": ((3, 8, 256, 128), BF16),
        "stat_out": ((3, 7, 8, 256), F32), "stat_in": ((3, 8, 8, 256), F32),
        "merged": ((3, 4, 64, 128), BF16), "merged_stat": ((3, 8, 256), F32),
        "land": ((3, 4, 64, 128), BF16), "land_stat": ((3, 4, 8, 256), F32),
        "home": ((2, 3, 2, 2, 32, 384), BF16), "own": ((2, 2, 3, 64, 128), BF16), "own_out": ((2, 3, 64, 128), BF16),
        "own_stat": ((2, 8, 128), F32), "w_all": ((2, 384, 3072), BF16), "att": ((2, 64, 768), BF16),
        "pair_out": ((4, 64, 768), BF16), "pair_in": ((4, 64, 768), BF16), "kept": ((4, 64, 768), F32),
        "bias_own": ((256, 1024), F32), "cols": ((256, 128), F32), "cols_own": ((128, 128), F32),
    }
    call = pl.pallas_call(
        kernel,
        out_shape=jax.ShapeDtypeStruct(inputs.shape, BF16),
        in_specs=[anywhere, anywhere, vmem, anywhere, vmem, vmem],
        out_specs=vmem,
        scratch_shapes=[pltpu.VMEM(*spec) for spec in buffers.values()] + [dma(shape) for shape in sems.values()],
        compiler_params=pltpu.CompilerParams(collective_id=0, has_side_effects=True, vmem_limit_bytes=48 << 20),
        name="stale_patch_attention",
    )
    return call(fresh, stale, text_mask.reshape(2, 128), out_weight, inputs, gate)


def solution(mesh):
    placed = (
        P(None, ("patch", "head"), None, None),
        P("patch", None, "head"),
        P(),
        P("head", None),
        P(None, ("patch", "head"), None),
        P(),
    )
    return jax.shard_map(
        shards,
        mesh=mesh,
        in_specs=placed,
        out_specs=P(None, ("patch", "head"), None),
        check_vma=False,
    )
```

```python
import functools

import jax
import jax.numpy as jnp
from jax import lax
from jax.experimental import pallas as pl
from jax.experimental.pallas import tpu as pltpu
from jax.sharding import PartitionSpec as P

HEAD_DIM = 128
MESH = pl.DeviceIdType.MESH
MASKED = -1e30
SCALE = HEAD_DIM**-0.5 * 1.4426950408889634
BF16 = jnp.bfloat16
F32 = jnp.float32


def device(x, y, z, c):
    return ((z // 2) * 16 + y * 4 + x, (z % 2) * 2 + c)


def plane(z):
    return (z // 2) % 2, 2 * (z % 2) + z // 4


def columns_of(rows):
    count, width = rows.shape
    padded = jnp.concatenate([rows, jnp.zeros((128 - count, width), F32)], axis=0)
    return jnp.transpose(padded)


def as_row(column, width):
    return jnp.transpose(jnp.broadcast_to(column, (width, 128)))[:8]


def attend(queries, keys, values, add_bias):
    scores = lax.dot_general(queries, keys, (((1,), (1,)), ((), ())), preferred_element_type=F32)
    scores = add_bias(scores)
    best = jnp.max(scores, axis=1, keepdims=True) * SCALE
    exps = jnp.exp2(scores * SCALE - best)
    total = jnp.sum(exps, axis=1, keepdims=True)
    summed = jnp.dot(exps.astype(BF16), values, preferred_element_type=F32)
    return (summed / total).astype(BF16), best + jnp.log2(total)


def kernel(
    fresh, stale_far, mask, weight, inputs_far, gate_far, out,
    inputs, gate, stale_raw, stale, q, kv, part_out, part_in, stat_out, stat_in, merged, att,
    home, own_out, own_in, own_stat_out, own_stat_in, w_all, near_out, near_in, kept, bias_own,
    zq_s, zq_r, zk_s, zs_s, zk_r, home_s, home_r, w_s, w_r, w_l, xq_s, xq_r, qf_s, qf_r, yk_s, yk_r,
    o_s, o_r, t_s, t_r, b_s, b_r, own_s, own_r, ot_s, ot_r, p_s, p_r, i_l,
):
    patch, head = lax.axis_index("patch"), lax.axis_index("head")
    x, y, zh = patch % 4, (patch // 4) % 4, patch // 16
    zl, c = head // 2, head % 2
    z = zh * 2 + zl
    step_here, group_here = plane(z)
    to_stale = pltpu.make_async_copy(stale_far, stale_raw, i_l.at[2])
    to_stale.start()
    sibling = device(x, y, z, 1 - c)

    def send(src, dst, ss, rs, to):
        pltpu.make_async_remote_copy(
            src_ref=src, dst_ref=dst, send_sem=ss, recv_sem=rs, device_id=to, device_id_type=MESH
        ).start()

    def wait(ref, sem):
        pltpu.make_async_copy(ref, ref, sem).wait()

    barrier = pltpu.get_barrier_semaphore()

    def greet(to):
        pl.semaphore_signal(barrier, inc=1, device_id=to, device_id_type=MESH)

    greet(sibling)

    @pl.loop(1, 8)
    def _(d):
        greet(device(x, y, (z + d) % 8, 0))
        greet(device(x, y, (z + d) % 8, 1))

    @pl.loop(1, 4)
    def _(d):
        greet(device((x + d) % 4, y, z, 0))
        greet(device((x + d) % 4, y, z, 1))
        greet(device(x, (y + d) % 4, z, c))

    to_stale.wait()
    for kind in range(2):
        stale[kind] = stale_raw[:, kind, :].reshape(2, 2, 32, 384)
    pl.semaphore_wait(barrier, 24)

    stale_plane = 4 * c + zl
    def spread(h):
        for lane in range(2):
            src = stale.at[:, :, lane, :, pl.ds(h * 128, 128)]
            dst = kv.at[h, :, y, pl.ds(2 * zh, 2)]
            here = jnp.logical_and(stale_plane == z, c == lane)

            @pl.when(here)
            def _():
                pltpu.make_async_copy(src, dst, zk_r.at[h]).start()

            @pl.when(jnp.logical_not(here))
            def _():
                send(src, dst, zs_s.at[h], zk_r.at[h], device(x, y, stale_plane, lane))

        def piece(of_step, kind, group):
            first = pl.multiple_of(group * 384 + h * 128, 128)
            return fresh.at[of_step, kind, :, pl.ds(first, 128)]

        @pl.when(step_here == 1)
        def _():
            pltpu.make_async_copy(piece(0, slice(1, 3), group_here), kv.at[h, :, y, z], zk_r.at[h]).start()

        pltpu.make_async_copy(piece(step_here, 0, group_here), q.at[h, c, 0, z], zq_r.at[h]).start()

        @pl.loop(1, 8)
        def _(d):
            to_z = (z + d) % 8
            to_step, to_group = plane(to_z)
            to = device(x, y, to_z, c)

            @pl.when(to_step == 1)
            def _():
                send(piece(0, slice(1, 3), to_group), kv.at[h, :, y, z], zk_s.at[h], zk_r.at[h], to)

            send(piece(to_step, 0, to_group), q.at[h, c, 0, z], zq_s.at[h], zq_r.at[h], to)

    spread(0)
    spread(1)

    pltpu.make_async_copy(weight, w_all.at[c], w_l.at[0]).start()
    pltpu.make_async_copy(inputs_far, inputs, i_l.at[0]).start()
    pltpu.make_async_copy(gate_far, gate, i_l.at[1]).start()
    send(weight, w_all.at[c], w_s.at[0], w_r.at[0], sibling)

    mask_row = jnp.where(x == 3, mask[1:2, :], mask[0:1, :])
    text = jnp.where(mask_row == 1, 0.0, MASKED)
    lanes = lax.broadcasted_iota(jnp.int32, (1, 128), 1)
    by_32, by_64, by_96 = (jnp.roll(text, shift, axis=1) for shift in (32, 64, 96))
    low = jnp.where(lanes < 96, by_64, by_32)
    high = jnp.where(lanes < 96, by_32, text)
    text_keys = jnp.where(jnp.logical_and(x >= 2, lanes >= 64), jnp.where(c == 0, low, high), 0.0)
    own_order = jnp.where(lanes < 32, text, jnp.where(lanes < 64, by_96, jnp.where(lanes < 96, by_32, text)))
    own_bias = jnp.where(jnp.logical_and(x >= 2, jnp.logical_and(y == 3, zh == 3)), own_order, 0.0)

    bias_own[...] = jnp.zeros((256, 1024), F32)
    bias_own[:, 896:1024] = jnp.broadcast_to(text_keys, (256, 128))
    same = lax.broadcasted_iota(jnp.int32, (256, 256), 0) // 64 == lax.broadcasted_iota(jnp.int32, (256, 256), 1) // 64
    own_cols = pl.ds(pl.multiple_of(y * 256, 256), 256)
    bias_own[:, own_cols] = jnp.where(same, MASKED, bias_own[:, own_cols])

    def gather(h):
        wait(kv.at[h, :, y], zk_r.at[h])

        @pl.loop(1, 4)
        def _(d):
            send(kv.at[h, :, y], kv.at[h, :, y], yk_s.at[h], yk_r.at[h, d - 1], device(x, (y + d) % 4, z, c))

        wait(q.at[h, c, 0], zq_r.at[h])

        @pl.loop(1, 4)
        def _(d):
            send(q.at[h, c, 0], q.at[h, c, 4 - d], xq_s.at[h], xq_r.at[h], device((x + d) % 4, y, z, c))

    gather(0)
    spread(2)
    gather(1)

    group = pl.multiple_of(head * 384, 128)
    pltpu.make_async_copy(fresh.at[:, :, :, pl.ds(group, 384)], home.at[:, :, c, zl], home_r.at[0]).start()

    @pl.loop(1, 4)
    def _(d):
        to_head = (head + d) % 4
        first = pl.multiple_of(to_head * 384, 128)
        send(fresh.at[:, :, :, pl.ds(first, 384)], home.at[:, :, c, zl], home_s.at[0], home_r.at[0], (patch, to_head))

    def pass_queries(h):
        wait(q.at[h, c, pl.ds(1, 3)], xq_r.at[h])
        send(q.at[h, c], q.at[h, c], qf_s.at[h], qf_r.at[h], sibling)

    pass_queries(0)
    gather(2)

    def attend_home():
        wait(home, home_r.at[0])
        for s in range(2):
            for h in range(3):
                rows = [home[s, kind, :, :, :, h * 128 : h * 128 + 128].reshape(128, 128) for kind in range(3)]
                block, lse = attend(*rows, lambda scores: scores + own_bias)
                lses = as_row(lse, 128)[:1]
                for lane in range(2):
                    own_out[s, lane, h] = block[lane * 64 : lane * 64 + 64]
                    own_stat_out[s, lane, h : h + 1, :] = lses if lane == 0 else jnp.roll(lses, 64, axis=1)
            for lane in range(2):
                to_z = 4 * c + 2 * s + zl
                here = jnp.logical_and(to_z == z, c == lane)
                to = device(x, y, to_z, lane)

                @pl.when(here)
                def _():
                    pltpu.make_async_copy(own_out.at[s, lane], own_in.at[:, zh], own_r.at[0]).start()
                    pltpu.make_async_copy(own_stat_out.at[s, lane], own_stat_in.at[zh], ot_r.at[0]).start()

                @pl.when(jnp.logical_not(here))
                def _():
                    send(own_out.at[s, lane], own_in.at[:, zh], own_s.at[0], own_r.at[0], to)
                    send(own_stat_out.at[s, lane], own_stat_in.at[zh], ot_s.at[0], ot_r.at[0], to)

    def attend_far(h):
        for d in range(1, 4):
            wait(kv.at[h, :, (y + 4 - d) % 4], yk_r.at[h, d - 1])
        wait(q.at[h, 1 - c], qf_r.at[h])

        def tile(r, lane, add_bias):
            keys, values = (kv[h, kind].reshape(1024, 128) for kind in range(2))
            return attend(q[h, lane, r].reshape(256, 128), keys, values, add_bias)

        def text_bias(scores):
            return jnp.concatenate([scores[:, :896], scores[:, 896:] + text_keys], axis=1)

        @pl.loop(2, 8)
        def _(index):
            r, lane = index // 2, index % 2
            block, lse = tile(r, lane, text_bias)
            part_out[h, index - 1] = block
            stat_out[h, index - 1] = as_row(lse, 256)
            to = device((x + r) % 4, y, z, lane)
            slot = (4 - r) * 2 + (c + lane) % 2
            send(part_out.at[h, index - 1], part_in.at[h, slot], o_s.at[h], o_r.at[h], to)
            send(stat_out.at[h, index - 1], stat_in.at[h, slot], t_s.at[h], t_r.at[h], to)

        block, lse = tile(0, 1 - c, lambda scores: scores + bias_own[...])
        part_out[h, 0] = block
        stat_out[h, 0] = as_row(lse, 256)
        send(part_out.at[h, 0], part_in.at[h, 1], o_s.at[h], o_r.at[h], sibling)
        send(stat_out.at[h, 0], stat_in.at[h, 1], t_s.at[h], t_r.at[h], sibling)
        block, lse = tile(0, c, lambda scores: scores + bias_own[...])
        part_in[h, 0] = block
        stat_in[h, 0] = as_row(lse, 256)

    def merge(h):
        wait(part_in.at[h, pl.ds(1, 7)], o_r.at[h])
        wait(stat_in.at[h, pl.ds(1, 7)], t_r.at[h])
        pairs = [jnp.where(lanes < 64, own_stat_in[2 * i, h : h + 1, :], jnp.roll(own_stat_in[2 * i + 1, h : h + 1, :], 64, axis=1)) for i in range(2)]
        stats = jnp.concatenate([stat_in[h, :, 0, :], jnp.concatenate(pairs, axis=1)], axis=0)
        shares = jnp.exp2(stats - jnp.max(stats, axis=0, keepdims=True))
        share_cols = columns_of(shares / jnp.sum(shares, axis=0, keepdims=True))
        summed = own_in[h].reshape(256, 128).astype(F32) * share_cols[:, 8:9]
        for i in range(8):
            summed = summed + part_in[h, i].astype(F32) * share_cols[:, i : i + 1]
        block = summed.astype(BF16)
        merged[h, 16:272] = block
        merged[h, 0:16] = block[240:256]
        merged[h, 272:288] = block[0:16]
        dst = att.at[step_here, group_here % 2, h]

        def window(to_z):
            return merged.at[h, pl.ds(pl.multiple_of(to_z * 32, 32), 64)]

        pltpu.make_async_copy(window(z), dst, b_r.at[h]).start()

        @pl.loop(1, 4)
        def _(d):
            to_z = (z + 2 * d) % 8
            send(window(to_z), dst, b_s.at[h], b_r.at[h], device(x, y, to_z, c))

    attend_far(0)
    pass_queries(1)
    attend_home()
    attend_far(1)
    pass_queries(2)
    wait(own_in, own_r.at[0])
    wait(own_stat_in, ot_r.at[0])
    merge(0)
    attend_far(2)
    merge(1)
    merge(2)

    wait(inputs, i_l.at[0])
    wait(gate, i_l.at[1])
    wait(weight, w_l.at[0])
    wait(weight, w_r.at[0])
    for h in range(3):
        wait(att.at[:, :, h], b_r.at[h])
    blocks = [jnp.concatenate([att[s, j, h] for j in range(2) for h in range(3)], axis=1) for s in range(2)]
    near = jnp.concatenate([block[rows] for rows in (slice(0, 16), slice(48, 64)) for block in blocks], axis=0)
    mine = jnp.concatenate([block[16:48] for block in blocks], axis=0)

    def project(rows, n):
        cut = slice(n * 768, n * 768 + 768)
        return sum(
            jnp.dot(rows[:, j * 384 : j * 384 + 384], w_all[j, :, cut], preferred_element_type=F32) for j in range(2)
        )

    for n in range(4):
        near_out[n] = project(near, n).astype(BF16).reshape(2, 2, 16, 768)
        send(near_out.at[n, 0], near_in.at[n, 1], p_s.at[n], p_r.at[n], device(x, y, (z + 7) % 8, c))
        send(near_out.at[n, 1], near_in.at[n, 0], p_s.at[n], p_r.at[n], device(x, y, (z + 1) % 8, c))
    for n in range(4):
        kept[n] = project(mine, n)
    for n in range(4):
        wait(near_in.at[n], p_r.at[n])
        cut = slice(n * 768, n * 768 + 768)
        for s in range(2):
            other = jnp.concatenate([near_in[n, 0, s], near_in[n, 1, s]], axis=0).astype(F32)
            branch = kept[n, s * 32 : s * 32 + 32] + other
            out[s, :, cut] = (inputs[s, :, cut].astype(F32) + gate[s : s + 1, cut] * branch).astype(BF16)

    for h in range(3):
        wait(q.at[h, 0, 0, pl.ds(0, 7)], zq_s.at[h])
        wait(q.at[h, 0, pl.ds(1, 3)], xq_s.at[h])
        wait(q.at[h, 0], qf_s.at[h])
        wait(kv.at[h, :, pl.ds(0, 3)], yk_s.at[h])
        wait(part_out.at[h, pl.ds(0, 7)], o_s.at[h])
        wait(stat_out.at[h, pl.ds(0, 7)], t_s.at[h])
        wait(merged.at[h, pl.ds(0, 192)], b_s.at[h])

        @pl.when(step_here == 1)
        def _():
            wait(kv.at[h, :, 0, pl.ds(0, 3)], zk_s.at[h])

        @pl.when(step_here == 0)
        def _():
            wait(kv.at[h, :, 0, pl.ds(0, 4)], zk_s.at[h])

        @pl.when(stale_plane == z)
        def _():
            wait(kv.at[h, :, 0, pl.ds(0, 2)], zs_s.at[h])

        @pl.when(stale_plane != z)
        def _():
            wait(kv.at[h, :, 0, pl.ds(0, 4)], zs_s.at[h])

    wait(home.at[:, :, 0], home_s.at[0])
    wait(home.at[:, :, 0, 0], home_s.at[0])
    wait(weight, w_s.at[0])

    @pl.when(zh // 2 == c)
    def _():
        wait(own_in.at[:, pl.ds(0, 3)], own_s.at[0])
        wait(own_stat_in.at[pl.ds(0, 3)], ot_s.at[0])

    @pl.when(zh // 2 != c)
    def _():
        wait(own_in, own_s.at[0])
        wait(own_stat_in, ot_s.at[0])

    for n in range(4):
        wait(near_out.at[n], p_s.at[n])


def shards(fresh_qkv, stale_kv, text_mask, out_weight, inputs, gate):
    fresh = jnp.transpose(fresh_qkv, (0, 2, 1, 3))
    vmem, anywhere = pl.BlockSpec(memory_space=pltpu.VMEM), pl.BlockSpec(memory_space=pl.ANY)
    dma = pltpu.SemaphoreType.DMA
    sems = {
        "zq_s": (3,), "zq_r": (3,), "zk_s": (3,), "zs_s": (3,), "zk_r": (3,), "home_s": (1,), "home_r": (1,),
        "w_s": (1,), "w_r": (1,), "w_l": (1,), "xq_s": (3,), "xq_r": (3,), "qf_s": (3,), "qf_r": (3,),
        "yk_s": (3,), "yk_r": (3, 3), "o_s": (3,), "o_r": (3,), "t_s": (3,), "t_r": (3,), "b_s": (3,), "b_r": (3,),
        "own_s": (1,), "own_r": (1,), "ot_s": (1,), "ot_r": (1,), "p_s": (4,), "p_r": (4,),
        "i_l": (3,),
    }
    buffers = {
        "inputs": ((2, 32, 3072), BF16), "gate": ((2, 3072), F32), "stale_raw": ((128, 2, 384), BF16),
        "stale": ((2, 2, 2, 32, 384), BF16),
        "q": ((3, 2, 4, 8, 32, 128), BF16), "kv": ((3, 2, 4, 8, 32, 128), BF16),
        "part_out": ((3, 7, 256, 128), BF16), "part_in": ((3, 8, 256, 128), BF16),
        "stat_out": ((3, 7, 8, 256), F32), "stat_in": ((3, 8, 8, 256), F32),
        "merged": ((3, 288, 128), BF16), "att": ((2, 2, 3, 64, 128), BF16),
        "home": ((2, 3, 2, 2, 32, 384), BF16), "own_out": ((2, 2, 3, 64, 128), BF16), "own_in": ((3, 4, 64, 128), BF16),
        "own_stat_out": ((2, 2, 8, 128), F32), "own_stat_in": ((4, 8, 128), F32), "w_all": ((2, 384, 3072), BF16),
        "near_out": ((4, 2, 2, 16, 768), BF16), "near_in": ((4, 2, 2, 16, 768), BF16), "kept": ((4, 64, 768), F32),
        "bias_own": ((256, 1024), F32),
    }
    call = pl.pallas_call(
        kernel,
        out_shape=jax.ShapeDtypeStruct(inputs.shape, BF16),
        in_specs=[anywhere, anywhere, vmem, anywhere, anywhere, anywhere],
        out_specs=vmem,
        scratch_shapes=[pltpu.VMEM(*spec) for spec in buffers.values()] + [dma(shape) for shape in sems.values()],
        compiler_params=pltpu.CompilerParams(collective_id=0, has_side_effects=True, vmem_limit_bytes=60 << 20),
        name="stale_patch_attention",
    )
    return call(fresh, stale_kv, text_mask.reshape(2, 128), out_weight, inputs, gate)


def solution(mesh):
    placed = (
        P(None, ("patch", "head"), None, None),
        P("patch", None, "head"),
        P(),
        P("head", None),
        P(None, ("patch", "head"), None),
        P(),
    )
    return jax.shard_map(
        shards,
        mesh=mesh,
        in_specs=placed,
        out_specs=P(None, ("patch", "head"), None),
        check_vma=False,
    )
```

```python
import functools

import jax
import jax.numpy as jnp
from jax import lax
from jax.experimental import pallas as pl
from jax.experimental.pallas import tpu as pltpu
from jax.sharding import PartitionSpec as P

HEAD_DIM = 128
MESH = pl.DeviceIdType.MESH
MASKED = -1e30
SCALE = HEAD_DIM**-0.5 * 1.4426950408889634
BF16 = jnp.bfloat16
F32 = jnp.float32


def device(x, y, z, c):
    return ((z // 2) * 16 + y * 4 + x, (z % 2) * 2 + c)


def plane(z):
    return (z // 2) % 2, 2 * (z % 2) + z // 4


def columns_of(rows):
    count, width = rows.shape
    padded = jnp.concatenate([rows, jnp.zeros((128 - count, width), F32)], axis=0)
    return jnp.transpose(padded)


def as_row(column, width):
    return jnp.transpose(jnp.broadcast_to(column, (width, 128)))[:8]


def score(queries, keys):
    return lax.dot_general(queries, keys, (((1,), (1,)), ((), ())), preferred_element_type=F32)


def weigh(scores, values):
    best = jnp.max(scores, axis=1, keepdims=True) * SCALE
    exps = jnp.exp2(scores * SCALE - best)
    total = jnp.sum(exps, axis=1, keepdims=True)
    summed = jnp.dot(exps.astype(BF16), values, preferred_element_type=F32)
    return summed / total, best + jnp.log2(total)


def kernel(
    fresh_far, stale_far, mask, weight, inputs_far, gate_far, out,
    inputs, gate, fresh, stale_raw, stale, q, kv, side_out, side_in, side_stat_out, side_stat_in, part_out, part_in, stat_out, stat_in, merged, att,
    home, own_out, own_in, own_stat_out, own_stat_in, w_all, near_out, near_in, kept, bias_own, held,
    zq_s, zq_r, zk_s, zs_s, zk_r, home_s, home_r, w_s, w_r, w_l, xq_s, xq_r, qf_s, qf_r, yk_s, yk_r, so_s, so_r, st_s, st_r,
    o_s, o_r, t_s, t_r, b_s, b_r, own_s, own_r, ot_s, ot_r, p_s, p_r, i_l,
):
    patch, head = lax.axis_index("patch"), lax.axis_index("head")
    x, y, zh = patch % 4, (patch // 4) % 4, patch // 16
    zl, c = head // 2, head % 2
    z = zh * 2 + zl
    step_here, group_here = plane(z)
    to_stale = pltpu.make_async_copy(stale_far, stale_raw, i_l.at[2])
    to_stale.start()
    to_fresh = pltpu.make_async_copy(fresh_far, fresh, i_l.at[3])
    to_fresh.start()
    sibling = device(x, y, z, 1 - c)

    def send(src, dst, ss, rs, to):
        pltpu.make_async_remote_copy(
            src_ref=src, dst_ref=dst, send_sem=ss, recv_sem=rs, device_id=to, device_id_type=MESH
        ).start()

    def wait(ref, sem):
        pltpu.make_async_copy(ref, ref, sem).wait()

    barrier = pltpu.get_barrier_semaphore()

    def greet(to):
        pl.semaphore_signal(barrier, inc=1, device_id=to, device_id_type=MESH)

    greet(sibling)

    @pl.loop(1, 8)
    def _(d):
        greet(device(x, y, (z + d) % 8, 0))
        greet(device(x, y, (z + d) % 8, 1))

    @pl.loop(1, 4)
    def _(d):
        greet(device((x + d) % 4, y, z, c))
        greet(device(x, (y + d) % 4, z, c))

    to_stale.wait()
    to_fresh.wait()
    for kind in range(2):
        stale[kind] = stale_raw[:, kind, :].reshape(2, 2, 32, 384)
    pl.semaphore_wait(barrier, 21)

    def query_peer(h, d):
        return device(x, (y + d) % 4, z, c) if h == 1 else device((x + d) % 4, y, z, c)

    def key_peer(h, d):
        return query_peer(1 - h % 2, d)

    def key_slot(h):
        return x if h == 1 else y

    stale_plane = 4 * c + zl
    def spread(h):
        for lane in range(2):
            src = stale.at[:, :, lane, :, pl.ds(h * 128, 128)]
            dst = kv.at[h, :, key_slot(h), pl.ds(2 * zh, 2)]
            here = jnp.logical_and(stale_plane == z, c == lane)

            @pl.when(here)
            def _():
                pltpu.make_async_copy(src, dst, zk_r.at[h]).start()

            @pl.when(jnp.logical_not(here))
            def _():
                send(src, dst, zs_s.at[h], zk_r.at[h], device(x, y, stale_plane, lane))

        def piece(of_step, kind, group):
            first = pl.multiple_of(group * 384 + h * 128, 128)
            return fresh.at[of_step, kind, :, pl.ds(first, 128)]

        @pl.when(step_here == 1)
        def _():
            pltpu.make_async_copy(piece(0, slice(1, 3), group_here), kv.at[h, :, key_slot(h), z], zk_r.at[h]).start()

        pltpu.make_async_copy(piece(step_here, 0, group_here), q.at[h, c, 0, z], zq_r.at[h]).start()

        @pl.loop(1, 8)
        def _(d):
            to_z = (z + d) % 8
            to_step, to_group = plane(to_z)
            to = device(x, y, to_z, c)

            @pl.when(to_step == 1)
            def _():
                send(piece(0, slice(1, 3), to_group), kv.at[h, :, key_slot(h), z], zk_s.at[h], zk_r.at[h], to)

        @pl.loop(1, 8)
        def _(d):
            to_z = (z + d) % 8
            to_step, to_group = plane(to_z)
            send(piece(to_step, 0, to_group), q.at[h, c, 0, z], zq_s.at[h], zq_r.at[h], device(x, y, to_z, c))

    spread(0)
    spread(1)
    spread(2)

    pltpu.make_async_copy(weight, w_all.at[c], w_l.at[0]).start()
    pltpu.make_async_copy(inputs_far, inputs, i_l.at[0]).start()
    pltpu.make_async_copy(gate_far, gate, i_l.at[1]).start()
    send(weight, w_all.at[c], w_s.at[0], w_r.at[0], sibling)

    text = jnp.where(mask[...] == 1, 0.0, MASKED)
    lanes = lax.broadcasted_iota(jnp.int32, (2, 128), 1)
    by_32, by_64, by_96 = (jnp.roll(text, shift, axis=1) for shift in (32, 64, 96))
    low = jnp.where(lanes < 96, by_64, by_32)
    high = jnp.where(lanes < 96, by_32, text)
    text_keys = jnp.where(lanes >= 64, jnp.where(c == 0, low, high), 0.0)
    of_column = jnp.where(x >= 2, jnp.where(x == 3, text_keys[1:2], text_keys[0:1]), 0.0)
    of_row = jnp.where(y == 3, text_keys, 0.0)
    far_biases = [[(7, of_column)], [(5, of_row[0:1]), (7, of_row[1:2])]]
    own_order = jnp.where(lanes < 32, text, jnp.where(lanes < 64, by_96, jnp.where(lanes < 96, by_32, text)))
    own_order = jnp.where(x == 3, own_order[1:2], own_order[0:1])
    own_bias = jnp.where(jnp.logical_and(x >= 2, jnp.logical_and(y == 3, zh == 3)), own_order, 0.0)

    def far_bias(h, scores):
        blocks = [scores[:, i * 128 : i * 128 + 128] for i in range(8)]
        for i, bias in far_biases[h % 2]:
            blocks[i] = blocks[i] + bias
        return jnp.concatenate(blocks, axis=1)

    same = lax.broadcasted_iota(jnp.int32, (256, 256), 0) // 64 == lax.broadcasted_iota(jnp.int32, (256, 256), 1) // 64
    for h in range(2):
        bias_own[h] = far_bias(h, jnp.zeros((256, 1024), F32))
        own_cols = pl.ds(pl.multiple_of(key_slot(h) * 256, 256), 256)
        bias_own[h, :, own_cols] = jnp.where(same, MASKED, bias_own[h, :, own_cols])

    def gather(h):
        slot = key_slot(h)
        wait(kv.at[h, :, slot], zk_r.at[h])

        @pl.loop(1, 4)
        def _(d):
            send(kv.at[h, :, slot], kv.at[h, :, slot], yk_s.at[h], yk_r.at[h, d - 1], key_peer(h, d))

        wait(q.at[h, c, 0], zq_r.at[h])

        @pl.loop(1, 4)
        def _(d):
            send(q.at[h, c, 0], q.at[h, c, 4 - d], xq_s.at[h], xq_r.at[h], query_peer(h, d))

    gather(0)
    gather(1)

    group = pl.multiple_of(head * 384, 128)
    pltpu.make_async_copy(fresh.at[:, :, :, pl.ds(group, 384)], home.at[:, :, c, zl], home_r.at[0]).start()

    @pl.loop(1, 4)
    def _(d):
        to_head = (head + d) % 4
        first = pl.multiple_of(to_head * 384, 128)
        send(fresh.at[:, :, :, pl.ds(first, 384)], home.at[:, :, c, zl], home_s.at[0], home_r.at[0], (patch, to_head))

    def pass_queries(h):
        wait(q.at[h, c, pl.ds(1, 3)], xq_r.at[h])
        send(q.at[h, c], q.at[h, c], qf_s.at[h], qf_r.at[h], sibling)

    pass_queries(0)
    gather(2)

    def attend_home():
        wait(home, home_r.at[0])
        for s in range(2):
            for h in range(3):
                rows = [home[s, kind, :, :, :, h * 128 : h * 128 + 128].reshape(128, 128) for kind in range(3)]
                block, lse = weigh(score(rows[0], rows[1]) + own_bias, rows[2])
                lses = as_row(lse, 128)[:1]
                for lane in range(2):
                    own_out[s, lane, h] = block[lane * 64 : lane * 64 + 64].astype(BF16)
                    own_stat_out[s, lane, h : h + 1, :] = lses if lane == 0 else jnp.roll(lses, 64, axis=1)
            for lane in range(2):
                to_z = 4 * c + 2 * s + zl
                here = jnp.logical_and(to_z == z, c == lane)
                to = device(x, y, to_z, lane)

                @pl.when(here)
                def _():
                    pltpu.make_async_copy(own_out.at[s, lane], own_in.at[:, zh], own_r.at[0]).start()
                    pltpu.make_async_copy(own_stat_out.at[s, lane], own_stat_in.at[zh], ot_r.at[0]).start()

                @pl.when(jnp.logical_not(here))
                def _():
                    send(own_out.at[s, lane], own_in.at[:, zh], own_s.at[0], own_r.at[0], to)
                    send(own_stat_out.at[s, lane], own_stat_in.at[zh], ot_s.at[0], ot_r.at[0], to)

    def attend_far(h):
        for d in range(1, 4):
            wait(kv.at[h, :, (key_slot(h) + 4 - d) % 4], yk_r.at[h, d - 1])
        wait(q.at[h, 1 - c], qf_r.at[h])

        tiles = [(r, lane) for lane in (1 - c, c) for r in (1, 2, 3, 0)]

        def score_tile(i):
            r, lane = tiles[i]
            scores = score(q[h, lane, r].reshape(256, 128), kv[h, 0].reshape(1024, 128))
            held[i % 2] = far_bias(h, scores) if r else scores + bias_own[h % 2]

        def join(r, block, lse):
            wait(side_in.at[h, r], so_r.at[h, r])
            wait(side_stat_in.at[h, r], st_r.at[h, r])
            lse_side = columns_of(side_stat_in[h, r])[:, :1]
            best = jnp.maximum(lse, lse_side)
            share, share_side = jnp.exp2(lse - best), jnp.exp2(lse_side - best)
            total = share + share_side
            block = (block * share + side_in[h, r].astype(F32) * share_side) / total
            return block.astype(BF16), as_row(best + jnp.log2(total), 256)

        score_tile(0)
        for i, (r, _) in enumerate(tiles):
            if i < 7:
                score_tile(i + 1)
            if i == 4 and h < 2:
                pass_queries(h + 1)
            block, lse = weigh(held[i % 2], kv[h, 1].reshape(1024, 128))
            if i < 4:
                side_out[h, r], side_stat_out[h, r] = block.astype(BF16), as_row(lse, 256)
                send(side_out.at[h, r], side_in.at[h, r], so_s.at[h], so_r.at[h, r], sibling)
                send(side_stat_out.at[h, r], side_stat_in.at[h, r], st_s.at[h], st_r.at[h, r], sibling)
            elif r:
                part_out[h, r - 1], stat_out[h, r - 1] = join(r, block, lse)
                send(part_out.at[h, r - 1], part_in.at[h, 4 - r], o_s.at[h], o_r.at[h], query_peer(h, r))
                send(stat_out.at[h, r - 1], stat_in.at[h, 4 - r], t_s.at[h], t_r.at[h], query_peer(h, r))
            else:
                part_in[h, 0], stat_in[h, 0] = join(r, block, lse)

    def merge(h):
        wait(part_in.at[h, pl.ds(1, 3)], o_r.at[h])
        wait(stat_in.at[h, pl.ds(1, 3)], t_r.at[h])
        first = lanes[:1] < 64
        pairs = [jnp.where(first, own_stat_in[2 * i, h : h + 1, :], jnp.roll(own_stat_in[2 * i + 1, h : h + 1, :], 64, axis=1)) for i in range(2)]
        stats = jnp.concatenate([stat_in[h, :, 0, :], jnp.concatenate(pairs, axis=1)], axis=0)
        shares = jnp.exp2(stats - jnp.max(stats, axis=0, keepdims=True))
        share_cols = columns_of(shares / jnp.sum(shares, axis=0, keepdims=True))
        summed = own_in[h].reshape(256, 128).astype(F32) * share_cols[:, 4:5]
        for i in range(4):
            summed = summed + part_in[h, i].astype(F32) * share_cols[:, i : i + 1]
        block = summed.astype(BF16)
        merged[h, 16:272] = block
        merged[h, 0:16] = block[240:256]
        merged[h, 272:288] = block[0:16]
        dst = att.at[step_here, group_here % 2, h]

        def window(to_z):
            return merged.at[h, pl.ds(pl.multiple_of(to_z * 32, 32), 64)]

        pltpu.make_async_copy(window(z), dst, b_r.at[h]).start()

        @pl.loop(1, 4)
        def _(d):
            to_z = (z + 2 * d) % 8
            send(window(to_z), dst, b_s.at[h], b_r.at[h], device(x, y, to_z, c))

    attend_far(0)
    attend_home()
    attend_far(1)
    attend_far(2)
    wait(own_in, own_r.at[0])
    wait(own_stat_in, ot_r.at[0])
    merge(0)
    merge(1)
    merge(2)

    wait(inputs, i_l.at[0])
    wait(gate, i_l.at[1])
    wait(weight, w_l.at[0])
    wait(weight, w_r.at[0])
    for h in range(3):
        wait(att.at[:, :, h], b_r.at[h])
    blocks = [jnp.concatenate([att[s, j, h] for j in range(2) for h in range(3)], axis=1) for s in range(2)]
    near = jnp.concatenate([block[rows] for rows in (slice(0, 16), slice(48, 64)) for block in blocks], axis=0)
    mine = jnp.concatenate([block[16:48] for block in blocks], axis=0)

    def project(rows, n):
        cut = slice(n * 768, n * 768 + 768)
        return sum(
            jnp.dot(rows[:, j * 384 : j * 384 + 384], w_all[j, :, cut], preferred_element_type=F32) for j in range(2)
        )

    for n in range(4):
        near_out[n] = project(near, n).astype(BF16).reshape(2, 2, 16, 768)
        send(near_out.at[n, 0], near_in.at[n, 1], p_s.at[n], p_r.at[n], device(x, y, (z + 7) % 8, c))
        send(near_out.at[n, 1], near_in.at[n, 0], p_s.at[n], p_r.at[n], device(x, y, (z + 1) % 8, c))
    for n in range(4):
        kept[n] = project(mine, n)
    for n in range(4):
        wait(near_in.at[n], p_r.at[n])
        cut = slice(n * 768, n * 768 + 768)
        for s in range(2):
            other = jnp.concatenate([near_in[n, 0, s], near_in[n, 1, s]], axis=0).astype(F32)
            branch = kept[n, s * 32 : s * 32 + 32] + other
            out[s, :, cut] = (inputs[s, :, cut].astype(F32) + gate[s : s + 1, cut] * branch).astype(BF16)

    for h in range(3):
        wait(q.at[h, 0, 0, pl.ds(0, 7)], zq_s.at[h])
        wait(q.at[h, 0, pl.ds(1, 3)], xq_s.at[h])
        wait(q.at[h, 0], qf_s.at[h])
        wait(kv.at[h, :, pl.ds(0, 3)], yk_s.at[h])
        wait(part_out.at[h], o_s.at[h])
        wait(stat_out.at[h], t_s.at[h])
        wait(side_out.at[h], so_s.at[h])
        wait(side_stat_out.at[h], st_s.at[h])
        wait(merged.at[h, pl.ds(0, 192)], b_s.at[h])

        @pl.when(step_here == 1)
        def _():
            wait(kv.at[h, :, 0, pl.ds(0, 3)], zk_s.at[h])

        @pl.when(step_here == 0)
        def _():
            wait(kv.at[h, :, 0, pl.ds(0, 4)], zk_s.at[h])

        @pl.when(stale_plane == z)
        def _():
            wait(kv.at[h, :, 0, pl.ds(0, 2)], zs_s.at[h])

        @pl.when(stale_plane != z)
        def _():
            wait(kv.at[h, :, 0, pl.ds(0, 4)], zs_s.at[h])

    wait(home.at[:, :, 0], home_s.at[0])
    wait(home.at[:, :, 0, 0], home_s.at[0])
    wait(weight, w_s.at[0])

    @pl.when(zh // 2 == c)
    def _():
        wait(own_in.at[:, pl.ds(0, 3)], own_s.at[0])
        wait(own_stat_in.at[pl.ds(0, 3)], ot_s.at[0])

    @pl.when(zh // 2 != c)
    def _():
        wait(own_in, own_s.at[0])
        wait(own_stat_in, ot_s.at[0])

    for n in range(4):
        wait(near_out.at[n], p_s.at[n])


def shards(fresh_qkv, stale_kv, text_mask, out_weight, inputs, gate):
    fresh = jnp.transpose(fresh_qkv, (0, 2, 1, 3))
    vmem, anywhere = pl.BlockSpec(memory_space=pltpu.VMEM), pl.BlockSpec(memory_space=pl.ANY)
    dma = pltpu.SemaphoreType.DMA
    sems = {
        "zq_s": (3,), "zq_r": (3,), "zk_s": (3,), "zs_s": (3,), "zk_r": (3,), "home_s": (1,), "home_r": (1,),
        "w_s": (1,), "w_r": (1,), "w_l": (1,), "xq_s": (3,), "xq_r": (3,), "qf_s": (3,), "qf_r": (3,),
        "yk_s": (3,), "yk_r": (3, 3), "so_s": (3,), "so_r": (3, 4), "st_s": (3,), "st_r": (3, 4), "o_s": (3,), "o_r": (3,), "t_s": (3,), "t_r": (3,), "b_s": (3,), "b_r": (3,),
        "own_s": (1,), "own_r": (1,), "ot_s": (1,), "ot_r": (1,), "p_s": (4,), "p_r": (4,),
        "i_l": (4,),
    }
    buffers = {
        "inputs": ((2, 32, 3072), BF16), "gate": ((2, 3072), F32), "fresh": ((2, 3, 32, 1536), BF16),
        "stale_raw": ((128, 2, 384), BF16),
        "stale": ((2, 2, 2, 32, 384), BF16),
        "q": ((3, 2, 4, 8, 32, 128), BF16), "kv": ((3, 2, 4, 8, 32, 128), BF16),
        "side_out": ((3, 4, 256, 128), BF16), "side_in": ((3, 4, 256, 128), BF16),
        "side_stat_out": ((3, 4, 8, 256), F32), "side_stat_in": ((3, 4, 8, 256), F32),
        "part_out": ((3, 3, 256, 128), BF16), "part_in": ((3, 4, 256, 128), BF16),
        "stat_out": ((3, 3, 8, 256), F32), "stat_in": ((3, 4, 8, 256), F32),
        "merged": ((3, 288, 128), BF16), "att": ((2, 2, 3, 64, 128), BF16),
        "home": ((2, 3, 2, 2, 32, 384), BF16), "own_out": ((2, 2, 3, 64, 128), BF16), "own_in": ((3, 4, 64, 128), BF16),
        "own_stat_out": ((2, 2, 8, 128), F32), "own_stat_in": ((4, 8, 128), F32), "w_all": ((2, 384, 3072), BF16),
        "near_out": ((4, 2, 2, 16, 768), BF16), "near_in": ((4, 2, 2, 16, 768), BF16), "kept": ((4, 64, 768), F32),
        "bias_own": ((2, 256, 1024), F32), "held": ((2, 256, 1024), F32),
    }
    call = pl.pallas_call(
        kernel,
        out_shape=jax.ShapeDtypeStruct(inputs.shape, BF16),
        in_specs=[anywhere, anywhere, vmem, anywhere, anywhere, anywhere],
        out_specs=vmem,
        scratch_shapes=[pltpu.VMEM(*spec) for spec in buffers.values()] + [dma(shape) for shape in sems.values()],
        compiler_params=pltpu.CompilerParams(collective_id=0, has_side_effects=True, vmem_limit_bytes=60 << 20),
        name="stale_patch_attention",
    )
    return call(fresh, stale_kv, text_mask.reshape(2, 128), out_weight, inputs, gate)


def solution(mesh):
    placed = (
        P(None, ("patch", "head"), None, None),
        P("patch", None, "head"),
        P(),
        P("head", None),
        P(None, ("patch", "head"), None),
        P(),
    )
    return jax.shard_map(
        shards,
        mesh=mesh,
        in_specs=placed,
        out_specs=P(None, ("patch", "head"), None),
        check_vma=False,
    )
```

```python
import functools

import jax
import jax.numpy as jnp
from jax import lax
from jax.experimental import pallas as pl
from jax.experimental.pallas import tpu as pltpu
from jax.sharding import PartitionSpec as P

HEAD_DIM = 128
MESH = pl.DeviceIdType.MESH
MASKED = -1e30
SCALE = HEAD_DIM**-0.5 * 1.4426950408889634
BF16 = jnp.bfloat16
F32 = jnp.float32


def device(x, y, z, c):
    return ((z // 2) * 16 + y * 4 + x, (z % 2) * 2 + c)


def plane(z):
    return (z // 2) % 2, 2 * (z % 2) + z // 4


def columns_of(rows):
    count, width = rows.shape
    padded = jnp.concatenate([rows, jnp.zeros((128 - count, width), F32)], axis=0)
    return jnp.transpose(padded)


def as_row(column, width):
    return jnp.transpose(jnp.broadcast_to(column, (width, 128)))[:8]


def score(queries, keys):
    return lax.dot_general(queries, keys, (((1,), (1,)), ((), ())), preferred_element_type=F32)


def weigh(scores, values):
    best = jnp.max(scores, axis=1, keepdims=True) * SCALE
    exps = jnp.exp2(scores * SCALE - best)
    total = jnp.sum(exps, axis=1, keepdims=True)
    summed = jnp.dot(exps.astype(BF16), values, preferred_element_type=F32)
    return summed / total, best + jnp.log2(total)


def kernel(
    fresh_far, stale_far, mask, weight, inputs_far, gate_far, out,
    inputs, gate, fresh, stale_raw, stale, q, kv, part_out, part_in, stat_out, stat_in, merged, att,
    home, own_out, own_in, own_stat_out, own_stat_in, w_all, near_out, near_in, kept, bias_own, held,
    zq_s, zq_r, zk_s, zs_s, zk_r, home_s, home_r, w_s, w_r, w_l, xq_s, xq_r, qf_s, qf_r, yk_s, yk_r,
    o_s, o_r, t_s, t_r, b_s, b_r, own_s, own_r, ot_s, ot_r, p_s, p_r, i_l,
):
    patch, head = lax.axis_index("patch"), lax.axis_index("head")
    x, y, zh = patch % 4, (patch // 4) % 4, patch // 16
    zl, c = head // 2, head % 2
    z = zh * 2 + zl
    step_here, group_here = plane(z)
    to_stale = pltpu.make_async_copy(stale_far, stale_raw, i_l.at[2])
    to_stale.start()
    to_fresh = pltpu.make_async_copy(fresh_far, fresh, i_l.at[3])
    to_fresh.start()
    sibling = device(x, y, z, 1 - c)

    def send(src, dst, ss, rs, to):
        pltpu.make_async_remote_copy(
            src_ref=src, dst_ref=dst, send_sem=ss, recv_sem=rs, device_id=to, device_id_type=MESH
        ).start()

    def wait(ref, sem):
        pltpu.make_async_copy(ref, ref, sem).wait()

    barrier = pltpu.get_barrier_semaphore()

    def greet(to):
        pl.semaphore_signal(barrier, inc=1, device_id=to, device_id_type=MESH)

    greet(sibling)

    @pl.loop(1, 8)
    def _(d):
        greet(device(x, y, (z + d) % 8, 0))
        greet(device(x, y, (z + d) % 8, 1))

    @pl.loop(1, 4)
    def _(d):
        for lane in range(2):
            greet(device((x + d) % 4, y, z, lane))
            greet(device(x, (y + d) % 4, z, lane))

    to_stale.wait()
    to_fresh.wait()
    for kind in range(2):
        stale[kind] = stale_raw[:, kind, :].reshape(2, 2, 32, 384)
    pl.semaphore_wait(barrier, 27)

    def query_peer(h, d, lane):
        return device(x, (y + d) % 4, z, lane) if h == 1 else device((x + d) % 4, y, z, lane)

    def key_peer(h, d):
        return query_peer(1 - h % 2, d, c)

    def key_slot(h):
        return x if h == 1 else y

    stale_plane = 4 * c + zl
    def spread(h):
        for lane in range(2):
            src = stale.at[:, :, lane, :, pl.ds(h * 128, 128)]
            dst = kv.at[h, :, key_slot(h), pl.ds(2 * zh, 2)]
            here = jnp.logical_and(stale_plane == z, c == lane)

            @pl.when(here)
            def _():
                pltpu.make_async_copy(src, dst, zk_r.at[h]).start()

            @pl.when(jnp.logical_not(here))
            def _():
                send(src, dst, zs_s.at[h], zk_r.at[h], device(x, y, stale_plane, lane))

        def piece(of_step, kind, group):
            first = pl.multiple_of(group * 384 + h * 128, 128)
            return fresh.at[of_step, kind, :, pl.ds(first, 128)]

        @pl.when(step_here == 1)
        def _():
            pltpu.make_async_copy(piece(0, slice(1, 3), group_here), kv.at[h, :, key_slot(h), z], zk_r.at[h]).start()

        pltpu.make_async_copy(piece(step_here, 0, group_here), q.at[h, c, 0, z], zq_r.at[h]).start()

        @pl.loop(1, 8)
        def _(d):
            to_z = (z + d) % 8
            to_step, to_group = plane(to_z)
            to = device(x, y, to_z, c)

            @pl.when(to_step == 1)
            def _():
                send(piece(0, slice(1, 3), to_group), kv.at[h, :, key_slot(h), z], zk_s.at[h], zk_r.at[h], to)

        @pl.loop(1, 8)
        def _(d):
            to_z = (z + d) % 8
            to_step, to_group = plane(to_z)
            send(piece(to_step, 0, to_group), q.at[h, c, 0, z], zq_s.at[h], zq_r.at[h], device(x, y, to_z, c))

    spread(0)
    spread(1)
    spread(2)

    pltpu.make_async_copy(weight, w_all.at[c], w_l.at[0]).start()
    pltpu.make_async_copy(inputs_far, inputs, i_l.at[0]).start()
    pltpu.make_async_copy(gate_far, gate, i_l.at[1]).start()
    send(weight, w_all.at[c], w_s.at[0], w_r.at[0], sibling)

    text = jnp.where(mask[...] == 1, 0.0, MASKED)
    lanes = lax.broadcasted_iota(jnp.int32, (2, 128), 1)
    by_32, by_64, by_96 = (jnp.roll(text, shift, axis=1) for shift in (32, 64, 96))
    low = jnp.where(lanes < 96, by_64, by_32)
    high = jnp.where(lanes < 96, by_32, text)
    text_keys = jnp.where(lanes >= 64, jnp.where(c == 0, low, high), 0.0)
    of_column = jnp.where(x >= 2, jnp.where(x == 3, text_keys[1:2], text_keys[0:1]), 0.0)
    of_row = jnp.where(y == 3, text_keys, 0.0)
    far_biases = [[(7, of_column)], [(5, of_row[0:1]), (7, of_row[1:2])]]
    own_order = jnp.where(lanes < 32, text, jnp.where(lanes < 64, by_96, jnp.where(lanes < 96, by_32, text)))
    own_order = jnp.where(x == 3, own_order[1:2], own_order[0:1])
    own_bias = jnp.where(jnp.logical_and(x >= 2, jnp.logical_and(y == 3, zh == 3)), own_order, 0.0)

    def far_bias(h, scores):
        blocks = [scores[:, i * 128 : i * 128 + 128] for i in range(8)]
        for i, bias in far_biases[h % 2]:
            blocks[i] = blocks[i] + bias
        return jnp.concatenate(blocks, axis=1)

    same = lax.broadcasted_iota(jnp.int32, (256, 256), 0) // 64 == lax.broadcasted_iota(jnp.int32, (256, 256), 1) // 64
    for h in range(2):
        bias_own[h] = far_bias(h, jnp.zeros((256, 1024), F32))
        own_cols = pl.ds(pl.multiple_of(key_slot(h) * 256, 256), 256)
        bias_own[h, :, own_cols] = jnp.where(same, MASKED, bias_own[h, :, own_cols])

    def gather(h):
        slot = key_slot(h)
        wait(kv.at[h, :, slot], zk_r.at[h])

        @pl.loop(1, 4)
        def _(d):
            send(kv.at[h, :, slot], kv.at[h, :, slot], yk_s.at[h], yk_r.at[h, d - 1], key_peer(h, d))

        wait(q.at[h, c, 0], zq_r.at[h])

        @pl.loop(1, 4)
        def _(d):
            send(q.at[h, c, 0], q.at[h, c, 4 - d], xq_s.at[h], xq_r.at[h], query_peer(h, d, c))

    gather(0)
    gather(1)

    group = pl.multiple_of(head * 384, 128)
    pltpu.make_async_copy(fresh.at[:, :, :, pl.ds(group, 384)], home.at[:, :, c, zl], home_r.at[0]).start()

    @pl.loop(1, 4)
    def _(d):
        to_head = (head + d) % 4
        first = pl.multiple_of(to_head * 384, 128)
        send(fresh.at[:, :, :, pl.ds(first, 384)], home.at[:, :, c, zl], home_s.at[0], home_r.at[0], (patch, to_head))

    def pass_queries(h):
        wait(q.at[h, c, pl.ds(1, 3)], xq_r.at[h])
        send(q.at[h, c], q.at[h, c], qf_s.at[h], qf_r.at[h], sibling)

    pass_queries(0)
    gather(2)

    def attend_home():
        wait(home, home_r.at[0])
        for s in range(2):
            for h in range(3):
                rows = [home[s, kind, :, :, :, h * 128 : h * 128 + 128].reshape(128, 128) for kind in range(3)]
                block, lse = weigh(score(rows[0], rows[1]) + own_bias, rows[2])
                lses = as_row(lse, 128)[:1]
                for lane in range(2):
                    own_out[s, lane, h] = block[lane * 64 : lane * 64 + 64].astype(BF16)
                    own_stat_out[s, lane, h : h + 1, :] = lses if lane == 0 else jnp.roll(lses, 64, axis=1)
            for lane in range(2):
                to_z = 4 * c + 2 * s + zl
                here = jnp.logical_and(to_z == z, c == lane)
                to = device(x, y, to_z, lane)

                @pl.when(here)
                def _():
                    pltpu.make_async_copy(own_out.at[s, lane], own_in.at[:, zh], own_r.at[0]).start()
                    pltpu.make_async_copy(own_stat_out.at[s, lane], own_stat_in.at[zh], ot_r.at[0]).start()

                @pl.when(jnp.logical_not(here))
                def _():
                    send(own_out.at[s, lane], own_in.at[:, zh], own_s.at[0], own_r.at[0], to)
                    send(own_stat_out.at[s, lane], own_stat_in.at[zh], ot_s.at[0], ot_r.at[0], to)

    def attend_far(h):
        for d in range(1, 4):
            wait(kv.at[h, :, (key_slot(h) + 4 - d) % 4], yk_r.at[h, d - 1])
        wait(q.at[h, 1 - c], qf_r.at[h])

        tiles = [(r, c if same else 1 - c, same) for r in (2, 1, 3) for same in (True, False)]
        tiles += [(0, 1 - c, False), (0, c, True)]

        def score_tile(i):
            r, lane, _ = tiles[i]
            scores = score(q[h, lane, r].reshape(256, 128), kv[h, 0].reshape(1024, 128))
            held[i % 2] = far_bias(h, scores) if r else scores + bias_own[h % 2]

        score_tile(0)
        for i, (r, lane, same) in enumerate(tiles):
            if i < 7:
                score_tile(i + 1)
            if i == 4 and h < 2:
                pass_queries(h + 1)
            block, lse = weigh(held[i % 2], kv[h, 1].reshape(1024, 128))
            block, lse = block.astype(BF16), as_row(lse, 256)
            if i == 7:
                part_in[h, 0], stat_in[h, 0] = block, lse
            else:
                part_out[h, i], stat_out[h, i] = block, lse
                slot = (4 - r) % 4 * 2 + (0 if same else 1)
                to = query_peer(h, r, lane) if r else sibling
                send(part_out.at[h, i], part_in.at[h, slot], o_s.at[h], o_r.at[h], to)
                send(stat_out.at[h, i], stat_in.at[h, slot], t_s.at[h], t_r.at[h], to)

    def merge(h):
        wait(part_in.at[h, pl.ds(1, 7)], o_r.at[h])
        wait(stat_in.at[h, pl.ds(1, 7)], t_r.at[h])
        first = lanes[:1] < 64
        pairs = [jnp.where(first, own_stat_in[2 * i, h : h + 1, :], jnp.roll(own_stat_in[2 * i + 1, h : h + 1, :], 64, axis=1)) for i in range(2)]
        stats = jnp.concatenate([stat_in[h, :, 0, :], jnp.concatenate(pairs, axis=1)], axis=0)
        shares = jnp.exp2(stats - jnp.max(stats, axis=0, keepdims=True))
        share_cols = columns_of(shares / jnp.sum(shares, axis=0, keepdims=True))
        summed = own_in[h].reshape(256, 128).astype(F32) * share_cols[:, 8:9]
        for i in range(8):
            summed = summed + part_in[h, i].astype(F32) * share_cols[:, i : i + 1]
        block = summed.astype(BF16)
        merged[h, 16:272] = block
        merged[h, 0:16] = block[240:256]
        merged[h, 272:288] = block[0:16]
        dst = att.at[step_here, group_here % 2, h]

        def window(to_z):
            return merged.at[h, pl.ds(pl.multiple_of(to_z * 32, 32), 64)]

        pltpu.make_async_copy(window(z), dst, b_r.at[h]).start()

        @pl.loop(1, 4)
        def _(d):
            to_z = (z + 2 * d) % 8
            send(window(to_z), dst, b_s.at[h], b_r.at[h], device(x, y, to_z, c))

    attend_far(0)
    attend_home()
    attend_far(1)
    attend_far(2)
    wait(own_in, own_r.at[0])
    wait(own_stat_in, ot_r.at[0])
    merge(0)
    merge(1)
    merge(2)

    wait(inputs, i_l.at[0])
    wait(gate, i_l.at[1])
    wait(weight, w_l.at[0])
    wait(weight, w_r.at[0])
    for h in range(3):
        wait(att.at[:, :, h], b_r.at[h])
    blocks = [jnp.concatenate([att[s, j, h] for j in range(2) for h in range(3)], axis=1) for s in range(2)]
    near = jnp.concatenate([block[rows] for rows in (slice(0, 16), slice(48, 64)) for block in blocks], axis=0)
    mine = jnp.concatenate([block[16:48] for block in blocks], axis=0)

    def project(rows, n):
        cut = slice(n * 768, n * 768 + 768)
        return sum(
            jnp.dot(rows[:, j * 384 : j * 384 + 384], w_all[j, :, cut], preferred_element_type=F32) for j in range(2)
        )

    for n in range(4):
        near_out[n] = project(near, n).astype(BF16).reshape(2, 2, 16, 768)
        send(near_out.at[n, 0], near_in.at[n, 1], p_s.at[n], p_r.at[n], device(x, y, (z + 7) % 8, c))
        send(near_out.at[n, 1], near_in.at[n, 0], p_s.at[n], p_r.at[n], device(x, y, (z + 1) % 8, c))
    for n in range(4):
        kept[n] = project(mine, n)
    for n in range(4):
        wait(near_in.at[n], p_r.at[n])
        cut = slice(n * 768, n * 768 + 768)
        for s in range(2):
            other = jnp.concatenate([near_in[n, 0, s], near_in[n, 1, s]], axis=0).astype(F32)
            branch = kept[n, s * 32 : s * 32 + 32] + other
            out[s, :, cut] = (inputs[s, :, cut].astype(F32) + gate[s : s + 1, cut] * branch).astype(BF16)

    for h in range(3):
        wait(q.at[h, 0, 0, pl.ds(0, 7)], zq_s.at[h])
        wait(q.at[h, 0, pl.ds(1, 3)], xq_s.at[h])
        wait(q.at[h, 0], qf_s.at[h])
        wait(kv.at[h, :, pl.ds(0, 3)], yk_s.at[h])
        wait(part_out.at[h], o_s.at[h])
        wait(stat_out.at[h], t_s.at[h])
        wait(merged.at[h, pl.ds(0, 192)], b_s.at[h])

        @pl.when(step_here == 1)
        def _():
            wait(kv.at[h, :, 0, pl.ds(0, 3)], zk_s.at[h])

        @pl.when(step_here == 0)
        def _():
            wait(kv.at[h, :, 0, pl.ds(0, 4)], zk_s.at[h])

        @pl.when(stale_plane == z)
        def _():
            wait(kv.at[h, :, 0, pl.ds(0, 2)], zs_s.at[h])

        @pl.when(stale_plane != z)
        def _():
            wait(kv.at[h, :, 0, pl.ds(0, 4)], zs_s.at[h])

    wait(home.at[:, :, 0], home_s.at[0])
    wait(home.at[:, :, 0, 0], home_s.at[0])
    wait(weight, w_s.at[0])

    @pl.when(zh // 2 == c)
    def _():
        wait(own_in.at[:, pl.ds(0, 3)], own_s.at[0])
        wait(own_stat_in.at[pl.ds(0, 3)], ot_s.at[0])

    @pl.when(zh // 2 != c)
    def _():
        wait(own_in, own_s.at[0])
        wait(own_stat_in, ot_s.at[0])

    for n in range(4):
        wait(near_out.at[n], p_s.at[n])


def shards(fresh_qkv, stale_kv, text_mask, out_weight, inputs, gate):
    fresh = jnp.transpose(fresh_qkv, (0, 2, 1, 3))
    vmem, anywhere = pl.BlockSpec(memory_space=pltpu.VMEM), pl.BlockSpec(memory_space=pl.ANY)
    dma = pltpu.SemaphoreType.DMA
    sems = {
        "zq_s": (3,), "zq_r": (3,), "zk_s": (3,), "zs_s": (3,), "zk_r": (3,), "home_s": (1,), "home_r": (1,),
        "w_s": (1,), "w_r": (1,), "w_l": (1,), "xq_s": (3,), "xq_r": (3,), "qf_s": (3,), "qf_r": (3,),
        "yk_s": (3,), "yk_r": (3, 3), "o_s": (3,), "o_r": (3,), "t_s": (3,), "t_r": (3,), "b_s": (3,), "b_r": (3,),
        "own_s": (1,), "own_r": (1,), "ot_s": (1,), "ot_r": (1,), "p_s": (4,), "p_r": (4,),
        "i_l": (4,),
    }
    buffers = {
        "inputs": ((2, 32, 3072), BF16), "gate": ((2, 3072), F32), "fresh": ((2, 3, 32, 1536), BF16),
        "stale_raw": ((128, 2, 384), BF16),
        "stale": ((2, 2, 2, 32, 384), BF16),
        "q": ((3, 2, 4, 8, 32, 128), BF16), "kv": ((3, 2, 4, 8, 32, 128), BF16),
        "part_out": ((3, 7, 256, 128), BF16), "part_in": ((3, 8, 256, 128), BF16),
        "stat_out": ((3, 7, 8, 256), F32), "stat_in": ((3, 8, 8, 256), F32),
        "merged": ((3, 288, 128), BF16), "att": ((2, 2, 3, 64, 128), BF16),
        "home": ((2, 3, 2, 2, 32, 384), BF16), "own_out": ((2, 2, 3, 64, 128), BF16), "own_in": ((3, 4, 64, 128), BF16),
        "own_stat_out": ((2, 2, 8, 128), F32), "own_stat_in": ((4, 8, 128), F32), "w_all": ((2, 384, 3072), BF16),
        "near_out": ((4, 2, 2, 16, 768), BF16), "near_in": ((4, 2, 2, 16, 768), BF16), "kept": ((4, 64, 768), F32),
        "bias_own": ((2, 256, 1024), F32), "held": ((2, 256, 1024), F32),
    }
    call = pl.pallas_call(
        kernel,
        out_shape=jax.ShapeDtypeStruct(inputs.shape, BF16),
        in_specs=[anywhere, anywhere, vmem, anywhere, anywhere, anywhere],
        out_specs=vmem,
        scratch_shapes=[pltpu.VMEM(*spec) for spec in buffers.values()] + [dma(shape) for shape in sems.values()],
        compiler_params=pltpu.CompilerParams(collective_id=0, has_side_effects=True, vmem_limit_bytes=60 << 20),
        name="stale_patch_attention",
    )
    return call(fresh, stale_kv, text_mask.reshape(2, 128), out_weight, inputs, gate)


def solution(mesh):
    placed = (
        P(None, ("patch", "head"), None, None),
        P("patch", None, "head"),
        P(),
        P("head", None),
        P(None, ("patch", "head"), None),
        P(),
    )
    return jax.shard_map(
        shards,
        mesh=mesh,
        in_specs=placed,
        out_specs=P(None, ("patch", "head"), None),
        check_vma=False,
    )
```
